32 devices in a mesh: obs: 4 (over x, core), state: 8 (over z, y).
Axes of the slice: x: 2, y: 2, z: 4, core: 2. Of those that a mesh axis runs over, the one named last changes fastest.
Arguments:
- jacobian: bfloat16 [8192, 10240], P('obs', 'state'), may hold values from -0.125 to 0.125
- obs_weight: float32 [8192], P('obs'), may hold values from 0.25 to 4
- observed: float32 [8192], P('obs'), may hold values from -6 to 6
- prior_state: bfloat16 [10240], P('state'), may hold values from -1.1953125 to 1.1953125
- prior_std: bfloat16 [10240], P('state'), may hold values from 0.5 to 2
- owner_slot: int32 [10240], P('state'), may hold values from 0 to 10239, each once
Outputs:
- gram_band: float32 [8, 1280, 3, 1280], P('state', 'obs')
- gradient: float32 [10240], P('state')
The draws below stay inside these ranges and needn't reach their ends.
Inputs may be any that keep to these rules, and one draw needn't show every extreme that they name: owner_slot names every position once.
All inputs are finite; a program needn't handle non-finite values.
Results may differ from the reference program's by a relative error of at most 0.0028.
Values may be sent and summed in bfloat16 or wider, within the bound.
A program may use at most 128 MiB of HBM per device.

```python
import math
import jax
import jax.numpy as jnp
from jax import lax

C = 1280
ROWS_DEV = 2048
ROWS = 8192
S = 10240
N_STATE = 8


def levels(rng, extent, split, smallest, largest):
    def one(dim, blocks):
        steps = jax.random.uniform(jax.random.fold_in(jax.random.fold_in(rng, 6), dim), (blocks,), jnp.float32, smallest / len(split), largest / len(split))
        return jnp.repeat(jnp.exp(steps), extent[dim] // blocks).reshape((-1,) + (1,) * (len(extent) - dim - 1))

    level = one(*split[0])
    for cut in split[1:]:
        level = level * one(*cut)
    return level


def bell_draw(key, dims, scale, limit, shards=(), held_as=jnp.bfloat16):
    drawn = scale * jax.random.normal(key, dims, jnp.float32)
    if shards:
        drawn = drawn * levels(key, dims, shards, -0.22, 0.18)
    return jnp.clip(drawn, -limit, limit).astype(held_as)


def setup_inputs(seed: int = 0) -> dict:
    arg_keys = jax.random.split(jax.random.key(seed), 7)
    jacobian = bell_draw(arg_keys[0], (ROWS, S), ROWS_DEV ** -0.5, 0.125, ((0, 4), (1, 8)))
    obs_weight = jnp.clip(jnp.exp(math.log(4.0) - 2.7725887 * jax.random.uniform(arg_keys[1], (ROWS,), jnp.float32) ** levels(arg_keys[1], (ROWS,), ((0, 4),), -0.2, 0.2)), 0.25, 4.0)
    observed = bell_draw(arg_keys[2], (ROWS,), 1.0, 6.0, ((0, 4),), jnp.float32)
    prior_state = bell_draw(arg_keys[3], (S,), 0.2, 1.1953125, ((0, 8),))
    prior_std = jnp.clip(jnp.exp(math.log(2.0) - 1.3862944 * jax.random.uniform(arg_keys[4], (S,), jnp.float32) ** levels(arg_keys[4], (S,), ((0, 8),), -0.2, 0.2)), 0.5, 2.0).astype(jnp.bfloat16)
    owner_slot = jax.random.permutation(arg_keys[5], S).astype(jnp.int32)
    return dict(jacobian=jacobian, obs_weight=obs_weight, observed=observed, prior_state=prior_state, prior_std=prior_std, owner_slot=owner_slot)


def reference(jacobian, obs_weight, observed, prior_state, prior_std, owner_slot):
    weighted = (jacobian * obs_weight[:, None]).astype(jnp.bfloat16)
    spread = prior_std.astype(jnp.float32)

    def one_block(block):
        left = lax.dynamic_slice_in_dim(weighted, (block * C).astype(jnp.int32), C, 1)
        rows_std = lax.dynamic_slice_in_dim(spread, (block * C).astype(jnp.int32), C, 0)
        parts = []
        for step in range(3):
            other = ((block + step) % N_STATE).astype(jnp.int32)
            right = lax.dynamic_slice_in_dim(jacobian, (other * C).astype(jnp.int32), C, 1)
            cols_std = lax.dynamic_slice_in_dim(spread, (other * C).astype(jnp.int32), C, 0)
            total = jnp.dot(left.T, right, preferred_element_type=jnp.float32)
            parts.append(total * rows_std[:, None] * cols_std[None, :])
        return jnp.stack(parts, axis=1)

    gram_band = lax.map(one_block, jnp.arange(N_STATE, dtype=jnp.int32))
    model = jnp.dot(jacobian, prior_state, preferred_element_type=jnp.float32)
    misfit = (obs_weight * (observed - model)).astype(jnp.bfloat16)
    descent = jnp.dot(misfit, jacobian, preferred_element_type=jnp.float32)
    gradient = jnp.zeros((S,), jnp.float32).at[owner_slot].set(spread * descent)
    return gram_band, gradient
```

```python
import functools

import jax
import jax.numpy as jnp
from jax import lax
from jax.experimental import pallas as pl
from jax.experimental.pallas import tpu as pltpu
from jax.sharding import PartitionSpec as P

MESH = pl.DeviceIdType.MESH
BF16 = jnp.bfloat16
F32 = jnp.float32
CHUNK = 256


def nn(left, right):
    return lax.dot_general(left, right, (((1,), (0,)), ((), ())), preferred_element_type=F32)


def nt(left, right):
    return lax.dot_general(left, right, (((1,), (1,)), ((), ())), preferred_element_type=F32)


def kernel(
    n_obs, n_state,
    jac, weight, observed, state, std_row, std_col, slot,
    band, gradient,
    cols, turned, far, near, csend, crecv, keep, xsend, xrecv,
    model, model_in, descent, descent_in, dense, dense_in, std_in,
    sem_local, sem_far, sem_near, sem_core, sem_x, sem_model, sem_descent, sem_dense, sem_std,
):
    group = lax.axis_index("obs")
    block = lax.axis_index("state")
    chunks, rows, wide = cols.shape
    quarter = band.shape[1]
    width = band.shape[2]
    units = 3 * chunks
    core = lax.rem(group, 2)
    side = group // 2
    other_core = {"obs": group + 1 - 2 * core}
    other_side = {"obs": lax.rem(group + 2, n_obs)}
    odd = lax.rem(block, 2)
    partner = {"state": block + 1 - 2 * odd}
    back_one = {"state": lax.rem(block + n_state - 1, n_state)}
    back_two = {"state": lax.rem(block + n_state - 2, n_state)}

    def remote(src, dst, sems, where, send, recv):
        return pltpu.make_async_remote_copy(
            src_ref=src, dst_ref=dst, send_sem=sems.at[0, send], recv_sem=sems.at[1, recv],
            device_id=where, device_id_type=MESH,
        )

    def local_copy(c):
        return pltpu.make_async_copy(
            jac.at[:, pl.ds(pl.multiple_of(c * wide, wide), wide)], cols.at[c], sem_local.at[c]
        )

    def far_copy(c):
        return remote(cols.at[c], far.at[c], sem_far, back_two, c, c)

    def near_copy(c, src):
        return remote(src.at[c], near.at[c], sem_near, partner, c, c)

    def core_copy(u):
        return remote(csend.at[u], crecv.at[u], sem_core, other_core, u, u)

    def side_copy(u):
        return remote(xsend.at[u], xrecv.at[u], sem_x, other_side, u, u)

    def each(count, body):
        def step(i, carry):
            body(i)
            return carry

        lax.fori_loop(0, count, step, 0)

    each(chunks, lambda c: local_copy(c).start())
    barrier = pltpu.get_barrier_semaphore()

    def greet_state(d):
        to = lax.rem(block + 1 + d, n_state)
        pl.semaphore_signal(barrier, inc=1, device_id={"state": to}, device_id_type=MESH)

    def greet_obs(d):
        to = lax.rem(group + 1 + d, n_obs)
        pl.semaphore_signal(barrier, inc=1, device_id={"obs": to}, device_id_type=MESH)

    each(n_state - 1, greet_state)
    each(n_obs - 1, greet_obs)
    pl.semaphore_wait(barrier, n_state - 1 + n_obs - 1)

    def launch(c):
        local_copy(c).wait()
        far_copy(c).start()

        @pl.when(odd == 1)
        def _():
            near_copy(c, cols).start()

    each(chunks, launch)
    std_near = remote(std_row, std_in.at[0], sem_std, back_one, 0, 0)
    std_far = remote(std_row, std_in.at[1], sem_std, back_two, 1, 1)
    std_near.start()
    std_far.start()

    parts = rows // wide

    def turn(i):
        c = i // parts
        r = pl.multiple_of(lax.rem(i, parts) * wide, wide)
        across = pl.ds(r, wide)
        down = pl.ds(pl.multiple_of(c * wide, wide), wide)
        tile = cols[c, across, :].astype(F32).T
        turned[down, across] = (tile * weight[:, across]).astype(BF16)
        lead = jnp.broadcast_to(state[:, down], (16, wide))
        piece = nn(lead, tile.astype(BF16))[:1]

        @pl.when(c == 0)
        def _():
            model[:, across] = piece

        @pl.when(c > 0)
        def _():
            model[:, across] += piece

    each(chunks * parts, turn)

    def model_copy(d):
        to = lax.rem(block + 1 + d, n_state)
        return remote(model, model_in.at[block], sem_model, {"state": to}, d, block)

    def model_landed(d):
        of = lax.rem(block + 1 + d, n_state)
        return remote(model, model_in.at[of], sem_model, {"state": of}, d, of)

    each(n_state - 1, lambda d: model_copy(d).start())

    def multiply(src, u):
        def given(h):
            q = 2 * h + 1 - core
            left = turned[pl.ds(pl.multiple_of(q * quarter, quarter), quarter), :]
            csend[u, h] = nn(left, src[...]).astype(BF16)

        def kept(h):
            q = 2 * h + core
            left = turned[pl.ds(pl.multiple_of(q * quarter, quarter), quarter), :]
            keep[u, h] = nn(left, src[...])

        each(2, given)
        core_copy(u).start()
        each(2, kept)

    def pass_on(u):
        core_copy(u).wait_recv()
        xsend[u] = (keep[u, 1 - side] + crecv[u, 1 - side].astype(F32)).astype(BF16)
        side_copy(u).start()
        keep[u, side] += crecv[u, side].astype(F32)

    my_rows = std_col[pl.ds(pl.multiple_of(group * quarter, quarter), quarter), :]

    def finish(u, k, c):
        side_copy(u).wait_recv()
        at = pl.ds(pl.multiple_of(c * wide, wide), wide)
        if k == 0:
            scale = std_row[:, at]
        else:
            scale = std_in[k - 1, :, at]
        band[k, :, at] = (keep[u, side] + xrecv[u].astype(F32)) * my_rows * scale

    def own(c):
        multiply(cols.at[c], c)

        @pl.when(c >= 1)
        def _():
            pass_on(c - 1)

        @pl.when(c >= 2)
        def _():
            finish(c - 2, 0, c - 2)

    each(chunks, own)

    def descent_copy(d):
        to = lax.rem(group + 1 + d, n_obs)
        return remote(descent, descent_in.at[group], sem_descent, {"obs": to}, d, group)

    def descent_landed(d):
        of = lax.rem(group + 1 + d, n_obs)
        return remote(descent, descent_in.at[of], sem_descent, {"obs": of}, d, of)

    def dense_copy(d):
        to = lax.rem(block + 1 + d, n_state)
        return remote(dense.at[to], dense_in.at[block], sem_dense, {"state": to}, d, block)

    def dense_landed(d):
        of = lax.rem(block + 1 + d, n_state)
        return remote(dense.at[of], dense_in.at[of], sem_dense, {"state": of}, d, of)

    def do_misfit():
        each(n_state - 1, lambda d: model_landed(d).wait_recv())
        model_in[block] = model[...]
        total = jnp.sum(model_in[...], axis=0)
        misfit = (weight[...] * (observed[...] - total)).astype(BF16)
        lead = jnp.broadcast_to(misfit, (16, rows))

        def part(c):
            at = pl.ds(pl.multiple_of(c * wide, wide), wide)
            descent[:, at] = nn(lead, cols[c])[:1]

        each(chunks, part)
        each(n_obs - 1, lambda d: descent_copy(d).start())

    def do_owners():
        each(n_obs - 1, lambda d: descent_landed(d).wait_recv())
        descent_in[group] = descent[...]
        scaled = std_row[...] * jnp.sum(descent_in[...], axis=0)
        high = scaled.astype(BF16).astype(F32)
        rest = scaled - high
        middle = rest.astype(BF16).astype(F32)
        low = rest - middle
        index = lax.broadcasted_iota(jnp.int32, (16, width), 0)
        three = jnp.where(
            index == 0, high, jnp.where(index == 1, middle, jnp.where(index == 2, low, 0.0))
        ).astype(BF16)
        place = lax.broadcasted_iota(jnp.int32, (wide, width), 0)

        def spread(i):
            t = i // chunks
            c = lax.rem(i, chunks)
            hot = jnp.where(slot[...] == place + i * wide, 1.0, 0.0).astype(BF16)
            at = pl.ds(pl.multiple_of(c * wide, wide), wide)
            dense[t, :, at] = jnp.sum(nt(three, hot), axis=0, keepdims=True)

        each(n_state * chunks, spread)
        each(n_state - 1, lambda d: dense_copy(d).start())

    def arrivals(j):
        @pl.when(j < chunks)
        def _():
            far_copy(j).wait_recv()

            @pl.when(odd == 0)
            def _():
                near_copy(j, far).start()

        @pl.when(j >= 1)
        def _():
            u = chunks + 2 * j - 1
            near_copy(j - 1, cols).wait_recv()
            multiply(near.at[j - 1], u)
            pass_on(u - 1)

            @pl.when(j >= 2)
            def _():
                finish(u - 2, 1, j - 2)

            @pl.when(j == 1)
            def _():
                finish(u - 2, 0, chunks - 1)
                std_near.wait_recv()
                std_far.wait_recv()

        @pl.when(j < chunks)
        def _():
            u = chunks + 2 * j
            multiply(far.at[j], u)
            pass_on(u - 1)

            @pl.when(j >= 1)
            def _():
                finish(u - 2, 2, j - 1)

            @pl.when(j == 0)
            def _():
                finish(u - 2, 0, chunks - 2)

        @pl.when(j == 1)
        def _():
            do_misfit()

        @pl.when(j == 2)
        def _():
            do_owners()

    each(chunks + 1, arrivals)
    pass_on(units - 1)
    each(n_state - 1, lambda d: dense_landed(d).wait_recv())
    dense_in[block] = dense[block]
    gradient[...] = jnp.sum(dense_in[...], axis=0)
    finish(units - 2, 2, chunks - 1)
    finish(units - 1, 1, chunks - 1)

    def sent(c):
        far_copy(c).wait_send()
        near_copy(c, cols).wait_send()

    each(chunks, sent)
    each(units, lambda u: core_copy(u).wait_send())
    each(units, lambda u: side_copy(u).wait_send())
    each(n_state - 1, lambda d: model_copy(d).wait_send())
    each(n_state - 1, lambda d: dense_copy(d).wait_send())
    each(n_obs - 1, lambda d: descent_copy(d).wait_send())
    std_near.wait_send()
    std_far.wait_send()


def on_device(n_obs, n_state, jacobian, obs_weight, observed, prior_state, prior_std, owner_slot):
    rows, width = jacobian.shape
    quarter = width // n_obs
    chunks = width // CHUNK
    units = 3 * chunks
    spread = prior_std.astype(F32)
    vmem = pl.BlockSpec(memory_space=pltpu.VMEM)
    dma = pltpu.SemaphoreType.DMA
    band, gradient = pl.pallas_call(
        functools.partial(kernel, n_obs, n_state),
        out_shape=(
            jax.ShapeDtypeStruct((3, quarter, width), F32),
            jax.ShapeDtypeStruct((1, width), F32),
        ),
        in_specs=[pl.BlockSpec(memory_space=pl.ANY)] + [vmem] * 6,
        out_specs=(vmem, vmem),
        scratch_shapes=[
            pltpu.VMEM((chunks, rows, CHUNK), BF16),
            pltpu.VMEM((width, rows), BF16),
            pltpu.VMEM((chunks, rows, CHUNK), BF16),
            pltpu.VMEM((chunks, rows, CHUNK), BF16),
            pltpu.VMEM((units, 2, quarter, CHUNK), BF16),
            pltpu.VMEM((units, 2, quarter, CHUNK), BF16),
            pltpu.VMEM((units, 2, quarter, CHUNK), F32),
            pltpu.VMEM((units, quarter, CHUNK), BF16),
            pltpu.VMEM((units, quarter, CHUNK), BF16),
            pltpu.VMEM((1, rows), F32),
            pltpu.VMEM((n_state, 1, rows), F32),
            pltpu.VMEM((1, width), F32),
            pltpu.VMEM((n_obs, 1, width), F32),
            pltpu.VMEM((n_state, 1, width), F32),
            pltpu.VMEM((n_state, 1, width), F32),
            pltpu.VMEM((2, 1, width), F32),
            dma((chunks,)),
            dma((2, chunks)),
            dma((2, chunks)),
            dma((2, units)),
            dma((2, units)),
            dma((2, n_state)),
            dma((2, n_obs)),
            dma((2, n_state)),
            dma((2, 2)),
        ],
        compiler_params=pltpu.CompilerParams(
            collective_id=0, has_side_effects=True, vmem_limit_bytes=60 * 1024 * 1024
        ),
        cost_estimate=pl.CostEstimate(
            flops=6 * rows * width * width, bytes_accessed=10 * rows * width, transcendentals=0
        ),
        name="band_and_gradient",
    )(
        jacobian, obs_weight[None, :], observed[None, :], prior_state[None, :],
        spread[None, :], spread[:, None], owner_slot[None, :],
    )
    return jnp.transpose(band, (1, 0, 2))[None], gradient[0]


def solution(mesh):
    n_obs, n_state = mesh.shape["obs"], mesh.shape["state"]
    assert n_obs == 4 and n_state % 2 == 0
    placed = (P("obs", "state"), P("obs"), P("obs"), P("state"), P("state"), P("state"))
    return jax.shard_map(
        functools.partial(on_device, n_obs, n_state),
        mesh=mesh,
        in_specs=placed,
        out_specs=(P("state", "obs", None, None), P("state")),
        check_vma=False,
    )
```

```python
import functools

import jax
import jax.numpy as jnp
from jax import lax
from jax.experimental import pallas as pl
from jax.experimental.pallas import tpu as pltpu
from jax.sharding import PartitionSpec as P

MESH = pl.DeviceIdType.MESH
BF16 = jnp.bfloat16
F32 = jnp.float32
CHUNK = 256


def nn(left, right):
    return lax.dot_general(left, right, (((1,), (0,)), ((), ())), preferred_element_type=F32)


def nt(left, right):
    return lax.dot_general(left, right, (((1,), (1,)), ((), ())), preferred_element_type=F32)


def kernel(
    n_obs, n_state,
    jac, weight, observed, rows_in,
    band, gradient,
    cols, turned, far, near, csend, crecv, keep, xsend, xrecv,
    model, model_in, descent, descent_in, dense, dense_in, std_in, std_row, std_col,
    sem_local, sem_far, sem_near, sem_core, sem_x, sem_model, sem_descent, sem_dense, sem_std,
):
    group = lax.axis_index("obs")
    block = lax.axis_index("state")
    chunks, rows, wide = cols.shape
    quarter = band.shape[1]
    width = band.shape[2]
    units = 3 * chunks
    core = lax.rem(group, 2)
    side = group // 2
    other_core = {"obs": group + 1 - 2 * core}
    other_side = {"obs": lax.rem(group + 2, n_obs)}
    odd = lax.rem(block, 2)
    partner = {"state": block + 1 - 2 * odd}
    back_one = {"state": lax.rem(block + n_state - 1, n_state)}
    back_two = {"state": lax.rem(block + n_state - 2, n_state)}

    def remote(src, dst, sems, where, send, recv):
        return pltpu.make_async_remote_copy(
            src_ref=src, dst_ref=dst, send_sem=sems.at[0, send], recv_sem=sems.at[1, recv],
            device_id=where, device_id_type=MESH,
        )

    def local_copy(c):
        return pltpu.make_async_copy(
            jac.at[:, pl.ds(pl.multiple_of(c * wide, wide), wide)], cols.at[c], sem_local.at[c]
        )

    def far_copy(c):
        return remote(cols.at[c], far.at[c], sem_far, back_two, c, c)

    def near_copy(c, src):
        return remote(src.at[c], near.at[c], sem_near, partner, c, c)

    def core_copy(u):
        return remote(csend.at[u], crecv.at[u], sem_core, other_core, u, u)

    def side_copy(u):
        return remote(xsend.at[u], xrecv.at[u], sem_x, other_side, u, u)

    def each(count, body):
        def step(i, carry):
            body(i)
            return carry

        lax.fori_loop(0, count, step, 0)

    each(chunks, lambda c: local_copy(c).start())
    std_row[...] = rows_in[1:2, :]
    barrier = pltpu.get_barrier_semaphore()

    def greet_state(d):
        to = lax.rem(block + 1 + d, n_state)
        pl.semaphore_signal(barrier, inc=1, device_id={"state": to}, device_id_type=MESH)

    def greet_obs(d):
        to = lax.rem(group + 1 + d, n_obs)
        pl.semaphore_signal(barrier, inc=1, device_id={"obs": to}, device_id_type=MESH)

    each(n_state - 1, greet_state)
    each(n_obs - 1, greet_obs)
    pl.semaphore_wait(barrier, n_state - 1 + n_obs - 1)

    def launch(c):
        far_copy(c).start()

        @pl.when(odd == 1)
        def _():
            near_copy(c, cols).start()

    local_copy(0).wait()
    launch(0)
    local_copy(1).wait()
    launch(1)
    each(chunks - 2, lambda c: local_copy(c + 2).wait())
    std_near = remote(std_row, std_in.at[0], sem_std, back_one, 0, 0)
    std_far = remote(std_row, std_in.at[1], sem_std, back_two, 1, 1)
    std_near.start()
    std_far.start()

    parts = rows // wide

    def turn(i):
        c = i // parts
        r = pl.multiple_of(lax.rem(i, parts) * wide, wide)
        across = pl.ds(r, wide)
        down = pl.ds(pl.multiple_of(c * wide, wide), wide)
        tile = cols[c, across, :].astype(F32).T
        turned[down, across] = (tile * weight[:, across]).astype(BF16)
        lead = jnp.broadcast_to(rows_in[0:1, down], (16, wide)).astype(BF16)
        piece = nn(lead, tile.astype(BF16))[:1]

        @pl.when(c == 0)
        def _():
            model[:, across] = piece

        @pl.when(c > 0)
        def _():
            model[:, across] += piece

    each(chunks * parts, turn)

    def upright(c):
        at = pl.ds(pl.multiple_of(c * wide, wide), wide)
        std_col[at, :] = jnp.broadcast_to(std_row[:, at], (std_col.shape[1], wide)).T

    each(chunks, upright)

    def model_copy(d):
        to = lax.rem(block + 1 + d, n_state)
        return remote(model, model_in.at[block], sem_model, {"state": to}, d, block)

    def model_landed(d):
        of = lax.rem(block + 1 + d, n_state)
        return remote(model, model_in.at[of], sem_model, {"state": of}, d, of)

    each(n_state - 1, lambda d: model_copy(d).start())

    def multiply(src, u):
        def given(h):
            q = 2 * h + 1 - core
            left = turned[pl.ds(pl.multiple_of(q * quarter, quarter), quarter), :]
            csend[u, h] = nn(left, src[...]).astype(BF16)

        def kept(h):
            q = 2 * h + core
            left = turned[pl.ds(pl.multiple_of(q * quarter, quarter), quarter), :]
            keep[u, h] = nn(left, src[...])

        each(2, given)
        core_copy(u).start()
        each(2, kept)

    def pass_on(u):
        core_copy(u).wait_recv()
        xsend[u] = (keep[u, 1 - side] + crecv[u, 1 - side].astype(F32)).astype(BF16)
        side_copy(u).start()
        keep[u, side] += crecv[u, side].astype(F32)

    my_rows = std_col[pl.ds(pl.multiple_of(group * quarter, quarter), quarter), 0:1]

    def finish(u, k, c):
        side_copy(u).wait_recv()
        at = pl.ds(pl.multiple_of(c * wide, wide), wide)
        if k == 0:
            scale = std_row[:, at]
        else:
            scale = std_in[k - 1, :, at]
        band[k, :, at] = (keep[u, side] + xrecv[u].astype(F32)) * my_rows * scale

    def descent_copy(d):
        to = lax.rem(group + 1 + d, n_obs)
        return remote(descent, descent_in.at[group], sem_descent, {"obs": to}, d, group)

    def descent_landed(d):
        of = lax.rem(group + 1 + d, n_obs)
        return remote(descent, descent_in.at[of], sem_descent, {"obs": of}, d, of)

    def dense_copy(d):
        to = lax.rem(block + 1 + d, n_state)
        return remote(dense.at[to], dense_in.at[block], sem_dense, {"state": to}, d, block)

    def dense_landed(d):
        of = lax.rem(block + 1 + d, n_state)
        return remote(dense.at[of], dense_in.at[of], sem_dense, {"state": of}, d, of)

    def do_misfit():
        each(n_state - 1, lambda d: model_landed(d).wait_recv())
        model_in[block] = model[...]
        total = jnp.sum(model_in[...], axis=0)
        misfit = (weight[...] * (observed[...] - total)).astype(BF16)
        lead = jnp.broadcast_to(misfit, (16, rows))

        def part(c):
            at = pl.ds(pl.multiple_of(c * wide, wide), wide)
            descent[:, at] = nn(lead, cols[c])[:1]

        each(chunks, part)
        each(n_obs - 1, lambda d: descent_copy(d).start())

    def do_owners():
        each(n_obs - 1, lambda d: descent_landed(d).wait_recv())
        descent_in[group] = descent[...]
        scaled = std_row[...] * jnp.sum(descent_in[...], axis=0)
        high = scaled.astype(BF16).astype(F32)
        rest = scaled - high
        middle = rest.astype(BF16).astype(F32)
        low = rest - middle
        index = lax.broadcasted_iota(jnp.int32, (16, width), 0)
        three = jnp.where(
            index == 0, high, jnp.where(index == 1, middle, jnp.where(index == 2, low, 0.0))
        ).astype(BF16)
        place = lax.broadcasted_iota(jnp.int32, (wide, width), 0)

        def spread(i):
            t = i // chunks
            c = lax.rem(i, chunks)
            hot = jnp.where(rows_in[2:3, :] == (place + i * wide).astype(F32), 1.0, 0.0).astype(BF16)
            at = pl.ds(pl.multiple_of(c * wide, wide), wide)
            dense[t, :, at] = jnp.sum(nt(three, hot), axis=0, keepdims=True)

        each(n_state * chunks, spread)
        each(n_state - 1, lambda d: dense_copy(d).start())

    def of_far(c):
        return 3 * c

    def of_own(c):
        return 3 * c + 1

    def of_near(c):
        return 3 * c + 2

    def arrivals(j):
        far_copy(j).wait_recv()

        @pl.when(odd == 0)
        def _():
            near_copy(j, far).start()

        @pl.when(j + 2 < chunks)
        def _():
            launch(j + 2)

        multiply(far.at[j], of_far(j))

        @pl.when(j == 0)
        def _():
            std_near.wait_recv()
            std_far.wait_recv()

        @pl.when(j == 1)
        def _():
            pass_on(of_own(0))

        @pl.when(j >= 2)
        def _():
            pass_on(of_near(j - 2))

        @pl.when(j >= 1)
        def _():
            finish(of_far(j - 1), 2, j - 1)

        multiply(cols.at[j], of_own(j))
        pass_on(of_far(j))

        @pl.when(j >= 1)
        def _():
            finish(of_own(j - 1), 0, j - 1)
            near_copy(j - 1, cols).wait_recv()
            multiply(near.at[j - 1], of_near(j - 1))
            pass_on(of_own(j))

        @pl.when(j >= 2)
        def _():
            finish(of_near(j - 2), 1, j - 2)

        @pl.when(j == 1)
        def _():
            do_misfit()

        @pl.when(j == 2)
        def _():
            do_owners()

    each(chunks, arrivals)
    last = chunks - 1
    pass_on(of_near(last - 1))
    finish(of_far(last), 2, last)
    finish(of_own(last), 0, last)
    each(n_state - 1, lambda d: dense_landed(d).wait_recv())
    dense_in[block] = dense[block]
    gradient[...] = jnp.sum(dense_in[...], axis=0)
    near_copy(last, cols).wait_recv()
    multiply(near.at[last], of_near(last))
    finish(of_near(last - 1), 1, last - 1)
    pass_on(of_near(last))
    finish(of_near(last), 1, last)

    def sent(c):
        far_copy(c).wait_send()
        near_copy(c, cols).wait_send()

    each(chunks, sent)
    each(units, lambda u: core_copy(u).wait_send())
    each(units, lambda u: side_copy(u).wait_send())
    each(n_state - 1, lambda d: model_copy(d).wait_send())
    each(n_state - 1, lambda d: dense_copy(d).wait_send())
    each(n_obs - 1, lambda d: descent_copy(d).wait_send())
    std_near.wait_send()
    std_far.wait_send()


def on_device(n_obs, n_state, jacobian, obs_weight, observed, prior_state, prior_std, owner_slot):
    rows, width = jacobian.shape
    quarter = width // n_obs
    chunks = width // CHUNK
    units = 3 * chunks
    vmem = pl.BlockSpec(memory_space=pltpu.VMEM)
    dma = pltpu.SemaphoreType.DMA
    band, gradient = pl.pallas_call(
        functools.partial(kernel, n_obs, n_state),
        out_shape=(
            jax.ShapeDtypeStruct((3, quarter, width), F32),
            jax.ShapeDtypeStruct((1, width), F32),
        ),
        in_specs=[pl.BlockSpec(memory_space=pl.ANY)] + [vmem] * 3,
        out_specs=(vmem, vmem),
        scratch_shapes=[
            pltpu.VMEM((chunks, rows, CHUNK), BF16),
            pltpu.VMEM((width, rows), BF16),
            pltpu.VMEM((chunks, rows, CHUNK), BF16),
            pltpu.VMEM((chunks, rows, CHUNK), BF16),
            pltpu.VMEM((units, 2, quarter, CHUNK), BF16),
            pltpu.VMEM((units, 2, quarter, CHUNK), BF16),
            pltpu.VMEM((units, 2, quarter, CHUNK), F32),
            pltpu.VMEM((units, quarter, CHUNK), BF16),
            pltpu.VMEM((units, quarter, CHUNK), BF16),
            pltpu.VMEM((1, rows), F32),
            pltpu.VMEM((n_state, 1, rows), F32),
            pltpu.VMEM((1, width), F32),
            pltpu.VMEM((n_obs, 1, width), F32),
            pltpu.VMEM((n_state, 1, width), F32),
            pltpu.VMEM((n_state, 1, width), F32),
            pltpu.VMEM((2, 1, width), F32),
            pltpu.VMEM((1, width), F32),
            pltpu.VMEM((width, 128), F32),
            dma((chunks,)),
            dma((2, chunks)),
            dma((2, chunks)),
            dma((2, units)),
            dma((2, units)),
            dma((2, n_state)),
            dma((2, n_obs)),
            dma((2, n_state)),
            dma((2, 2)),
        ],
        compiler_params=pltpu.CompilerParams(
            collective_id=0, has_side_effects=True, vmem_limit_bytes=60 * 1024 * 1024
        ),
        cost_estimate=pl.CostEstimate(
            flops=6 * rows * width * width, bytes_accessed=10 * rows * width, transcendentals=0
        ),
        name="band_and_gradient",
    )(
        jacobian, obs_weight[None, :], observed[None, :],
        jnp.stack([prior_state.astype(F32), prior_std.astype(F32), owner_slot.astype(F32)]),
    )
    return jnp.transpose(band, (1, 0, 2))[None], gradient[0]


def solution(mesh):
    n_obs, n_state = mesh.shape["obs"], mesh.shape["state"]
    assert n_obs == 4 and n_state % 2 == 0
    placed = (P("obs", "state"), P("obs"), P("obs"), P("state"), P("state"), P("state"))
    return jax.shard_map(
        functools.partial(on_device, n_obs, n_state),
        mesh=mesh,
        in_specs=placed,
        out_specs=(P("state", "obs", None, None), P("state")),
        check_vma=False,
    )
```

```python
import functools

import jax
import jax.numpy as jnp
from jax import lax
from jax.experimental import pallas as pl
from jax.experimental.pallas import tpu as pltpu
from jax.sharding import PartitionSpec as P

MESH = pl.DeviceIdType.MESH
BF16 = jnp.bfloat16
F32 = jnp.float32
CHUNK = 256


def nn(left, right):
    return lax.dot_general(left, right, (((1,), (0,)), ((), ())), preferred_element_type=F32)


def nt(left, right):
    return lax.dot_general(left, right, (((1,), (1,)), ((), ())), preferred_element_type=F32)


def kernel(
    n_obs, n_state,
    jac, weight, observed, rows_in,
    band, gradient,
    cols, turned, far, near, csend, crecv, keep, xsend, xrecv,
    model, model_in, descent, descent_in, dense, dense_in, std_in, std_row, std_col,
    sem_local, sem_far, sem_near, sem_core, sem_x, sem_model, sem_descent, sem_dense, sem_std,
):
    group = lax.axis_index("obs")
    block = lax.axis_index("state")
    chunks, rows, wide = cols.shape
    quarter = band.shape[1]
    width = band.shape[2]
    units = 3 * chunks
    core = lax.rem(group, 2)
    side = group // 2
    other_core = {"obs": group + 1 - 2 * core}
    other_side = {"obs": lax.rem(group + 2, n_obs)}
    odd = lax.rem(block, 2)
    partner = {"state": block + 1 - 2 * odd}
    back_one = {"state": lax.rem(block + n_state - 1, n_state)}
    back_two = {"state": lax.rem(block + n_state - 2, n_state)}

    def remote(src, dst, sems, where, send, recv):
        return pltpu.make_async_remote_copy(
            src_ref=src, dst_ref=dst, send_sem=sems.at[0, send], recv_sem=sems.at[1, recv],
            device_id=where, device_id_type=MESH,
        )

    def local_copy(c):
        return pltpu.make_async_copy(
            jac.at[:, pl.ds(pl.multiple_of(c * wide, wide), wide)], cols.at[c], sem_local.at[c]
        )

    def far_copy(c):
        return remote(cols.at[c], far.at[c], sem_far, back_two, c, c)

    def near_copy(c, src):
        return remote(src.at[c], near.at[c], sem_near, partner, c, c)

    def core_copy(u):
        return remote(csend.at[u], crecv.at[u], sem_core, other_core, u, u)

    def side_copy(u):
        return remote(xsend.at[u], xrecv.at[u], sem_x, other_side, u, u)

    def each(count, body):
        def step(i, carry):
            body(i)
            return carry

        lax.fori_loop(0, count, step, 0)

    each(chunks, lambda c: local_copy(c).start())
    std_row[...] = rows_in[1:2, :]
    barrier = pltpu.get_barrier_semaphore()

    def greet_state(d):
        to = lax.rem(block + 1 + d, n_state)
        pl.semaphore_signal(barrier, inc=1, device_id={"state": to}, device_id_type=MESH)

    def greet_obs(d):
        to = lax.rem(group + 1 + d, n_obs)
        pl.semaphore_signal(barrier, inc=1, device_id={"obs": to}, device_id_type=MESH)

    each(n_state - 1, greet_state)
    each(n_obs - 1, greet_obs)
    pl.semaphore_wait(barrier, n_state - 1 + n_obs - 1)

    def launch(c):
        far_copy(c).start()

        @pl.when(odd == 1)
        def _():
            near_copy(c, cols).start()

    local_copy(0).wait()
    launch(0)
    local_copy(1).wait()
    launch(1)
    each(chunks - 2, lambda c: local_copy(c + 2).wait())
    std_near = remote(std_row, std_in.at[0], sem_std, back_one, 0, 0)
    std_far = remote(std_row, std_in.at[1], sem_std, back_two, 1, 1)
    std_near.start()
    std_far.start()

    parts = rows // wide

    def turn(i):
        c = i // parts
        r = pl.multiple_of(lax.rem(i, parts) * wide, wide)
        across = pl.ds(r, wide)
        down = pl.ds(pl.multiple_of(c * wide, wide), wide)
        tile = cols[c, across, :].astype(F32).T
        turned[down, across] = (tile * weight[:, across]).astype(BF16)
        lead = jnp.broadcast_to(rows_in[0:1, down], (16, wide)).astype(BF16)
        piece = nn(lead, tile.astype(BF16))[:1]

        @pl.when(c == 0)
        def _():
            model[:, across] = piece

        @pl.when(c > 0)
        def _():
            model[:, across] += piece

    each(chunks * parts, turn)

    def upright(c):
        at = pl.ds(pl.multiple_of(c * wide, wide), wide)
        std_col[at, :] = jnp.broadcast_to(std_row[:, at], (std_col.shape[1], wide)).T

    each(chunks, upright)

    def model_copy(d):
        to = lax.rem(block + 1 + d, n_state)
        return remote(model, model_in.at[block], sem_model, {"state": to}, d, block)

    def model_landed(d):
        of = lax.rem(block + 1 + d, n_state)
        return remote(model, model_in.at[of], sem_model, {"state": of}, d, of)

    each(n_state - 1, lambda d: model_copy(d).start())

    def multiply(src, u):
        def given(h):
            q = 2 * h + 1 - core
            left = turned[pl.ds(pl.multiple_of(q * quarter, quarter), quarter), :]
            csend[u, h] = nn(left, src[...]).astype(BF16)

        def kept(h):
            q = 2 * h + core
            left = turned[pl.ds(pl.multiple_of(q * quarter, quarter), quarter), :]
            keep[u, h] = nn(left, src[...])

        each(2, given)
        core_copy(u).start()
        each(2, kept)

    def pass_on(u):
        core_copy(u).wait_recv()
        xsend[u] = (keep[u, 1 - side] + crecv[u, 1 - side].astype(F32)).astype(BF16)
        side_copy(u).start()
        keep[u, side] += crecv[u, side].astype(F32)

    my_rows = std_col[pl.ds(pl.multiple_of(group * quarter, quarter), quarter), 0:1]

    def finish(u, k, c):
        side_copy(u).wait_recv()
        at = pl.ds(pl.multiple_of(c * wide, wide), wide)
        if k == 0:
            scale = std_row[:, at]
        else:
            scale = std_in[k - 1, :, at]
        band[k, :, at] = (keep[u, side] + xrecv[u].astype(F32)) * my_rows * scale

    def descent_copy(d):
        to = lax.rem(group + 1 + d, n_obs)
        return remote(descent, descent_in.at[group], sem_descent, {"obs": to}, d, group)

    def descent_landed(d):
        of = lax.rem(group + 1 + d, n_obs)
        return remote(descent, descent_in.at[of], sem_descent, {"obs": of}, d, of)

    def dense_copy(d):
        to = lax.rem(block + 1 + d, n_state)
        return remote(dense.at[to], dense_in.at[block], sem_dense, {"state": to}, d, block)

    def dense_landed(d):
        of = lax.rem(block + 1 + d, n_state)
        return remote(dense.at[of], dense_in.at[of], sem_dense, {"state": of}, d, of)

    def do_misfit():
        each(n_state - 1, lambda d: model_landed(d).wait_recv())
        model_in[block] = model[...]
        total = jnp.sum(model_in[...], axis=0)
        misfit = (weight[...] * (observed[...] - total)).astype(BF16)
        lead = jnp.broadcast_to(misfit, (16, rows))

        def part(c):
            at = pl.ds(pl.multiple_of(c * wide, wide), wide)
            descent[:, at] = nn(lead, cols[c])[:1]

        each(chunks, part)
        each(n_obs - 1, lambda d: descent_copy(d).start())

    def do_owners():
        each(n_obs - 1, lambda d: descent_landed(d).wait_recv())
        descent_in[group] = descent[...]
        scaled = std_row[...] * jnp.sum(descent_in[...], axis=0)
        high = scaled.astype(BF16).astype(F32)
        rest = scaled - high
        middle = rest.astype(BF16).astype(F32)
        low = rest - middle
        index = lax.broadcasted_iota(jnp.int32, (16, width), 0)
        three = jnp.where(
            index == 0, high, jnp.where(index == 1, middle, jnp.where(index == 2, low, 0.0))
        ).astype(BF16)
        place = lax.broadcasted_iota(jnp.int32, (wide, width), 0)

        def spread(i):
            t = i // chunks
            c = lax.rem(i, chunks)
            hot = jnp.where(rows_in[2:3, :] == (place + i * wide).astype(F32), 1.0, 0.0).astype(BF16)
            at = pl.ds(pl.multiple_of(c * wide, wide), wide)
            dense[t, :, at] = jnp.sum(nt(three, hot), axis=0, keepdims=True)

        each(n_state * chunks, spread)
        each(n_state - 1, lambda d: dense_copy(d).start())

    def of_far(c):
        return 3 * c

    def of_own(c):
        return 3 * c + 1

    def of_near(c):
        return 3 * c + 2

    def arrivals(j):
        far_copy(j).wait_recv()

        @pl.when(odd == 0)
        def _():
            near_copy(j, far).start()


        multiply(far.at[j], of_far(j))

        @pl.when(j == 0)
        def _():
            std_near.wait_recv()
            std_far.wait_recv()

        @pl.when(j == 1)
        def _():
            pass_on(of_own(0))

        @pl.when(j >= 2)
        def _():
            pass_on(of_near(j - 2))

        @pl.when(j >= 1)
        def _():
            finish(of_far(j - 1), 2, j - 1)

        @pl.when(j + 4 < chunks)
        def _():
            far_copy(j + 2).wait_send()
            launch(j + 4)

        multiply(cols.at[j], of_own(j))
        pass_on(of_far(j))

        @pl.when(j >= 1)
        def _():
            finish(of_own(j - 1), 0, j - 1)
            near_copy(j - 1, cols).wait_recv()
            multiply(near.at[j - 1], of_near(j - 1))
            pass_on(of_own(j))

        @pl.when(j >= 2)
        def _():
            finish(of_near(j - 2), 1, j - 2)

        @pl.when(j == 0)
        def _():
            do_owners()

    def follow(c):
        far_copy(c).wait_send()
        launch(c + 2)

    do_misfit()
    each(2, follow)
    each(chunks, arrivals)
    last = chunks - 1
    pass_on(of_near(last - 1))
    finish(of_far(last), 2, last)
    finish(of_own(last), 0, last)
    each(n_state - 1, lambda d: dense_landed(d).wait_recv())
    dense_in[block] = dense[block]
    gradient[...] = jnp.sum(dense_in[...], axis=0)
    near_copy(last, cols).wait_recv()
    multiply(near.at[last], of_near(last))
    finish(of_near(last - 1), 1, last - 1)
    pass_on(of_near(last))
    finish(of_near(last), 1, last)

    def sent(c):
        near_copy(c, cols).wait_send()

    each(chunks, sent)
    far_copy(chunks - 2).wait_send()
    far_copy(chunks - 1).wait_send()
    each(units, lambda u: core_copy(u).wait_send())
    each(units, lambda u: side_copy(u).wait_send())
    each(n_state - 1, lambda d: model_copy(d).wait_send())
    each(n_state - 1, lambda d: dense_copy(d).wait_send())
    each(n_obs - 1, lambda d: descent_copy(d).wait_send())
    std_near.wait_send()
    std_far.wait_send()


def on_device(n_obs, n_state, jacobian, obs_weight, observed, prior_state, prior_std, owner_slot):
    rows, width = jacobian.shape
    quarter = width // n_obs
    chunks = width // CHUNK
    units = 3 * chunks
    vmem = pl.BlockSpec(memory_space=pltpu.VMEM)
    dma = pltpu.SemaphoreType.DMA
    band, gradient = pl.pallas_call(
        functools.partial(kernel, n_obs, n_state),
        out_shape=(
            jax.ShapeDtypeStruct((3, quarter, width), F32),
            jax.ShapeDtypeStruct((1, width), F32),
        ),
        in_specs=[pl.BlockSpec(memory_space=pl.ANY)] + [vmem] * 3,
        out_specs=(vmem, vmem),
        scratch_shapes=[
            pltpu.VMEM((chunks, rows, CHUNK), BF16),
            pltpu.VMEM((width, rows), BF16),
            pltpu.VMEM((chunks, rows, CHUNK), BF16),
            pltpu.VMEM((chunks, rows, CHUNK), BF16),
            pltpu.VMEM((units, 2, quarter, CHUNK), BF16),
            pltpu.VMEM((units, 2, quarter, CHUNK), BF16),
            pltpu.VMEM((units, 2, quarter, CHUNK), F32),
            pltpu.VMEM((units, quarter, CHUNK), BF16),
            pltpu.VMEM((units, quarter, CHUNK), BF16),
            pltpu.VMEM((1, rows), F32),
            pltpu.VMEM((n_state, 1, rows), F32),
            pltpu.VMEM((1, width), F32),
            pltpu.VMEM((n_obs, 1, width), F32),
            pltpu.VMEM((n_state, 1, width), F32),
            pltpu.VMEM((n_state, 1, width), F32),
            pltpu.VMEM((2, 1, width), F32),
            pltpu.VMEM((1, width), F32),
            pltpu.VMEM((width, 128), F32),
            dma((chunks,)),
            dma((2, chunks)),
            dma((2, chunks)),
            dma((2, units)),
            dma((2, units)),
            dma((2, n_state)),
            dma((2, n_obs)),
            dma((2, n_state)),
            dma((2, 2)),
        ],
        compiler_params=pltpu.CompilerParams(
            collective_id=0, has_side_effects=True, vmem_limit_bytes=60 * 1024 * 1024
        ),
        cost_estimate=pl.CostEstimate(
            flops=6 * rows * width * width, bytes_accessed=10 * rows * width, transcendentals=0
        ),
        name="band_and_gradient",
    )(
        jacobian, obs_weight[None, :], observed[None, :],
        jnp.stack([prior_state.astype(F32), prior_std.astype(F32), owner_slot.astype(F32)]),
    )
    return jnp.transpose(band, (1, 0, 2))[None], gradient[0]


def solution(mesh):
    n_obs, n_state = mesh.shape["obs"], mesh.shape["state"]
    assert n_obs == 4 and n_state % 2 == 0
    placed = (P("obs", "state"), P("obs"), P("obs"), P("state"), P("state"), P("state"))
    return jax.shard_map(
        functools.partial(on_device, n_obs, n_state),
        mesh=mesh,
        in_specs=placed,
        out_specs=(P("state", "obs", None, None), P("state")),
        check_vma=False,
    )
```

```python
import functools

import jax
import jax.numpy as jnp
from jax import lax
from jax.experimental import pallas as pl
from jax.experimental.pallas import tpu as pltpu
from jax.sharding import PartitionSpec as P

MESH = pl.DeviceIdType.MESH
BF16 = jnp.bfloat16
F32 = jnp.float32
CHUNK = 256


def nn(left, right):
    return lax.dot_general(left, right, (((1,), (0,)), ((), ())), preferred_element_type=F32)


def nt(left, right):
    return lax.dot_general(left, right, (((1,), (1,)), ((), ())), preferred_element_type=F32)


def kernel(
    n_obs, n_state,
    jac, weight, observed, rows_in,
    band, gradient,
    cols, turned, far, near, csend, crecv, keep, xsend, xrecv,
    model, model_in, descent, descent_in, dense, dense_in, std_in, std_row, std_col,
    sem_local, sem_far, sem_near, sem_core, sem_x, sem_model, sem_descent, sem_dense, sem_std,
):
    group = lax.axis_index("obs")
    block = lax.axis_index("state")
    chunks, rows, wide = cols.shape
    quarter = band.shape[1]
    width = band.shape[2]
    units = 3 * chunks
    core = lax.rem(group, 2)
    side = group // 2
    other_core = {"obs": group + 1 - 2 * core}
    other_side = {"obs": lax.rem(group + 2, n_obs)}
    odd = lax.rem(block, 2)
    partner = {"state": block + 1 - 2 * odd}
    back_one = {"state": lax.rem(block + n_state - 1, n_state)}
    back_two = {"state": lax.rem(block + n_state - 2, n_state)}

    def remote(src, dst, sems, where, send, recv):
        return pltpu.make_async_remote_copy(
            src_ref=src, dst_ref=dst, send_sem=sems.at[0, send], recv_sem=sems.at[1, recv],
            device_id=where, device_id_type=MESH,
        )

    def local_copy(c):
        return pltpu.make_async_copy(
            jac.at[:, pl.ds(pl.multiple_of(c * wide, wide), wide)], cols.at[c], sem_local.at[c]
        )

    def far_copy(c):
        return remote(cols.at[c], far.at[c], sem_far, back_two, c, c)

    def near_copy(c, src):
        return remote(src.at[c], near.at[c], sem_near, partner, c, c)

    def core_copy(u):
        return remote(csend.at[u], crecv.at[u], sem_core, other_core, u, u)

    def side_copy(u):
        return remote(xsend.at[u], xrecv.at[u], sem_x, other_side, u, u)

    def each(count, body):
        def step(i, carry):
            body(i)
            return carry

        lax.fori_loop(0, count, step, 0)

    each(chunks, lambda c: local_copy(c).start())
    std_row[...] = rows_in[1:2, :]
    barrier = pltpu.get_barrier_semaphore()

    def greet_state(d):
        to = lax.rem(block + 1 + d, n_state)
        pl.semaphore_signal(barrier, inc=1, device_id={"state": to}, device_id_type=MESH)

    def greet_obs(d):
        to = lax.rem(group + 1 + d, n_obs)
        pl.semaphore_signal(barrier, inc=1, device_id={"obs": to}, device_id_type=MESH)

    each(n_state - 1, greet_state)
    each(n_obs - 1, greet_obs)
    pl.semaphore_wait(barrier, n_state - 1 + n_obs - 1)

    def launch(c):
        far_copy(c).start()

        @pl.when(odd == 1)
        def _():
            near_copy(c, cols).start()

    local_copy(0).wait()
    launch(0)
    local_copy(1).wait()
    each(chunks - 2, lambda c: local_copy(c + 2).wait())
    std_near = remote(std_row, std_in.at[0], sem_std, back_one, 0, 0)
    std_far = remote(std_row, std_in.at[1], sem_std, back_two, 1, 1)
    std_near.start()
    std_far.start()

    parts = rows // wide

    def turn(i):
        c = i // parts
        r = pl.multiple_of(lax.rem(i, parts) * wide, wide)
        across = pl.ds(r, wide)
        down = pl.ds(pl.multiple_of(c * wide, wide), wide)
        tile = cols[c, across, :].astype(F32).T
        turned[down, across] = (tile * weight[:, across]).astype(BF16)
        lead = jnp.broadcast_to(rows_in[0:1, down], (16, wide)).astype(BF16)
        piece = nn(lead, tile.astype(BF16))[:1]

        @pl.when(c == 0)
        def _():
            model[:, across] = piece

        @pl.when(c > 0)
        def _():
            model[:, across] += piece

    each(chunks * parts, turn)

    def upright(c):
        at = pl.ds(pl.multiple_of(c * wide, wide), wide)
        std_col[at, :] = jnp.broadcast_to(std_row[:, at], (std_col.shape[1], wide)).T

    each(chunks, upright)

    def model_copy(d):
        to = lax.rem(block + 1 + d, n_state)
        return remote(model, model_in.at[block], sem_model, {"state": to}, d, block)

    def model_landed(d):
        of = lax.rem(block + 1 + d, n_state)
        return remote(model, model_in.at[of], sem_model, {"state": of}, d, of)

    each(n_state - 1, lambda d: model_copy(d).start())

    def multiply(src, u):
        def given(h):
            q = 2 * h + 1 - core
            left = turned[pl.ds(pl.multiple_of(q * quarter, quarter), quarter), :]
            csend[u, h] = nn(left, src[...]).astype(BF16)

        def kept(h):
            q = 2 * h + core
            left = turned[pl.ds(pl.multiple_of(q * quarter, quarter), quarter), :]
            keep[u, h] = nn(left, src[...])

        each(2, given)
        core_copy(u).start()
        each(2, kept)

    def pass_on(u):
        core_copy(u).wait_recv()
        xsend[u] = (keep[u, 1 - side] + crecv[u, 1 - side].astype(F32)).astype(BF16)
        side_copy(u).start()
        keep[u, side] += crecv[u, side].astype(F32)

    my_rows = std_col[pl.ds(pl.multiple_of(group * quarter, quarter), quarter), 0:1]

    def finish(u, k, c):
        side_copy(u).wait_recv()
        at = pl.ds(pl.multiple_of(c * wide, wide), wide)
        if k == 0:
            scale = std_row[:, at]
        else:
            scale = std_in[k - 1, :, at]
        band[k, :, at] = (keep[u, side] + xrecv[u].astype(F32)) * my_rows * scale

    def descent_copy(d):
        to = lax.rem(group + 1 + d, n_obs)
        return remote(descent, descent_in.at[group], sem_descent, {"obs": to}, d, group)

    def descent_landed(d):
        of = lax.rem(group + 1 + d, n_obs)
        return remote(descent, descent_in.at[of], sem_descent, {"obs": of}, d, of)

    def dense_copy(d):
        to = lax.rem(block + 1 + d, n_state)
        return remote(dense.at[to], dense_in.at[block], sem_dense, {"state": to}, d, block)

    def dense_landed(d):
        of = lax.rem(block + 1 + d, n_state)
        return remote(dense.at[of], dense_in.at[of], sem_dense, {"state": of}, d, of)

    def do_misfit():
        each(n_state - 1, lambda d: model_landed(d).wait_recv())
        model_in[block] = model[...]
        total = jnp.sum(model_in[...], axis=0)
        misfit = (weight[...] * (observed[...] - total)).astype(BF16)
        lead = jnp.broadcast_to(misfit, (16, rows))

        def part(c):
            at = pl.ds(pl.multiple_of(c * wide, wide), wide)
            descent[:, at] = nn(lead, cols[c])[:1]

        each(chunks, part)
        each(n_obs - 1, lambda d: descent_copy(d).start())

    def do_owners():
        each(n_obs - 1, lambda d: descent_landed(d).wait_recv())
        descent_in[group] = descent[...]
        scaled = std_row[...] * jnp.sum(descent_in[...], axis=0)
        high = scaled.astype(BF16).astype(F32)
        rest = scaled - high
        middle = rest.astype(BF16).astype(F32)
        low = rest - middle
        index = lax.broadcasted_iota(jnp.int32, (16, width), 0)
        three = jnp.where(
            index == 0, high, jnp.where(index == 1, middle, jnp.where(index == 2, low, 0.0))
        ).astype(BF16)
        place = lax.broadcasted_iota(jnp.int32, (wide, width), 0)

        def spread(i):
            t = i // chunks
            c = lax.rem(i, chunks)
            hot = jnp.where(rows_in[2:3, :] == (place + i * wide).astype(F32), 1.0, 0.0).astype(BF16)
            at = pl.ds(pl.multiple_of(c * wide, wide), wide)
            dense[t, :, at] = jnp.sum(nt(three, hot), axis=0, keepdims=True)

        each(n_state * chunks, spread)
        each(n_state - 1, lambda d: dense_copy(d).start())

    def of_far(c):
        return 3 * c

    def of_own(c):
        return 3 * c + 1

    def of_near(c):
        return 3 * c + 2

    def arrivals(j):
        far_copy(j).wait_send()

        @pl.when(j + 1 < chunks)
        def _():
            launch(j + 1)

        far_copy(j).wait_recv()

        @pl.when(odd == 0)
        def _():
            near_copy(j, far).start()


        multiply(far.at[j], of_far(j))

        @pl.when(j == 0)
        def _():
            std_near.wait_recv()
            std_far.wait_recv()

        @pl.when(j == 1)
        def _():
            pass_on(of_own(0))

        @pl.when(j >= 2)
        def _():
            pass_on(of_near(j - 2))

        @pl.when(j >= 1)
        def _():
            finish(of_far(j - 1), 2, j - 1)

        multiply(cols.at[j], of_own(j))
        pass_on(of_far(j))

        @pl.when(j >= 1)
        def _():
            finish(of_own(j - 1), 0, j - 1)
            near_copy(j - 1, cols).wait_recv()
            multiply(near.at[j - 1], of_near(j - 1))
            pass_on(of_own(j))

        @pl.when(j >= 2)
        def _():
            finish(of_near(j - 2), 1, j - 2)

        @pl.when(j == 0)
        def _():
            do_misfit()

        @pl.when(j == 1)
        def _():
            do_owners()

    each(chunks, arrivals)
    last = chunks - 1
    pass_on(of_near(last - 1))
    finish(of_far(last), 2, last)
    finish(of_own(last), 0, last)
    each(n_state - 1, lambda d: dense_landed(d).wait_recv())
    dense_in[block] = dense[block]
    gradient[...] = jnp.sum(dense_in[...], axis=0)
    near_copy(last, cols).wait_recv()
    multiply(near.at[last], of_near(last))
    finish(of_near(last - 1), 1, last - 1)
    pass_on(of_near(last))
    finish(of_near(last), 1, last)

    def sent(c):
        near_copy(c, cols).wait_send()

    each(chunks, sent)
    each(units, lambda u: core_copy(u).wait_send())
    each(units, lambda u: side_copy(u).wait_send())
    each(n_state - 1, lambda d: model_copy(d).wait_send())
    each(n_state - 1, lambda d: dense_copy(d).wait_send())
    each(n_obs - 1, lambda d: descent_copy(d).wait_send())
    std_near.wait_send()
    std_far.wait_send()


def on_device(n_obs, n_state, jacobian, obs_weight, observed, prior_state, prior_std, owner_slot):
    rows, width = jacobian.shape
    quarter = width // n_obs
    chunks = width // CHUNK
    units = 3 * chunks
    vmem = pl.BlockSpec(memory_space=pltpu.VMEM)
    dma = pltpu.SemaphoreType.DMA
    band, gradient = pl.pallas_call(
        functools.partial(kernel, n_obs, n_state),
        out_shape=(
            jax.ShapeDtypeStruct((3, quarter, width), F32),
            jax.ShapeDtypeStruct((1, width), F32),
        ),
        in_specs=[pl.BlockSpec(memory_space=pl.ANY)] + [vmem] * 3,
        out_specs=(vmem, vmem),
        scratch_shapes=[
            pltpu.VMEM((chunks, rows, CHUNK), BF16),
            pltpu.VMEM((width, rows), BF16),
            pltpu.VMEM((chunks, rows, CHUNK), BF16),
            pltpu.VMEM((chunks, rows, CHUNK), BF16),
            pltpu.VMEM((units, 2, quarter, CHUNK), BF16),
            pltpu.VMEM((units, 2, quarter, CHUNK), BF16),
            pltpu.VMEM((units, 2, quarter, CHUNK), F32),
            pltpu.VMEM((units, quarter, CHUNK), BF16),
            pltpu.VMEM((units, quarter, CHUNK), BF16),
            pltpu.VMEM((1, rows), F32),
            pltpu.VMEM((n_state, 1, rows), F32),
            pltpu.VMEM((1, width), F32),
            pltpu.VMEM((n_obs, 1, width), F32),
            pltpu.VMEM((n_state, 1, width), F32),
            pltpu.VMEM((n_state, 1, width), F32),
            pltpu.VMEM((2, 1, width), F32),
            pltpu.VMEM((1, width), F32),
            pltpu.VMEM((width, 128), F32),
            dma((chunks,)),
            dma((2, chunks)),
            dma((2, chunks)),
            dma((2, units)),
            dma((2, units)),
            dma((2, n_state)),
            dma((2, n_obs)),
            dma((2, n_state)),
            dma((2, 2)),
        ],
        compiler_params=pltpu.CompilerParams(
            collective_id=0, has_side_effects=True, vmem_limit_bytes=60 * 1024 * 1024
        ),
        cost_estimate=pl.CostEstimate(
            flops=6 * rows * width * width, bytes_accessed=10 * rows * width, transcendentals=0
        ),
        name="band_and_gradient",
    )(
        jacobian, obs_weight[None, :], observed[None, :],
        jnp.stack([prior_state.astype(F32), prior_std.astype(F32), owner_slot.astype(F32)]),
    )
    return jnp.transpose(band, (1, 0, 2))[None], gradient[0]


def solution(mesh):
    n_obs, n_state = mesh.shape["obs"], mesh.shape["state"]
    assert n_obs == 4 and n_state % 2 == 0
    placed = (P("obs", "state"), P("obs"), P("obs"), P("state"), P("state"), P("state"))
    return jax.shard_map(
        functools.partial(on_device, n_obs, n_state),
        mesh=mesh,
        in_specs=placed,
        out_specs=(P("state", "obs", None, None), P("state")),
        check_vma=False,
    )
```

```python
import functools

import jax
import jax.numpy as jnp
from jax import lax
from jax.experimental import pallas as pl
from jax.experimental.pallas import tpu as pltpu
from jax.sharding import PartitionSpec as P

MESH = pl.DeviceIdType.MESH
BF16 = jnp.bfloat16
F32 = jnp.float32
CHUNK = 256


def nn(left, right):
    return lax.dot_general(left, right, (((1,), (0,)), ((), ())), preferred_element_type=F32)


def nt(left, right):
    return lax.dot_general(left, right, (((1,), (1,)), ((), ())), preferred_element_type=F32)


def kernel(
    n_obs, n_state,
    jac, weight, observed, rows_in,
    band, gradient,
    cols, turned, far, near, csend, crecv, keep, xsend, xrecv,
    model, model_in, descent, descent_in, dense, dense_in, std_in, std_row, std_col,
    sem_local, sem_far, sem_near, sem_core, sem_x, sem_model, sem_descent, sem_dense, sem_std,
):
    group = lax.axis_index("obs")
    block = lax.axis_index("state")
    chunks, rows, wide = cols.shape
    quarter = band.shape[1]
    width = band.shape[2]
    units = 3 * chunks
    core = lax.rem(group, 2)
    side = group // 2
    other_core = {"obs": group + 1 - 2 * core}
    other_side = {"obs": lax.rem(group + 2, n_obs)}
    odd = lax.rem(block, 2)
    partner = {"state": block + 1 - 2 * odd}
    back_one = {"state": lax.rem(block + n_state - 1, n_state)}
    back_two = {"state": lax.rem(block + n_state - 2, n_state)}

    def remote(src, dst, sems, where, send, recv):
        return pltpu.make_async_remote_copy(
            src_ref=src, dst_ref=dst, send_sem=sems.at[0, send], recv_sem=sems.at[1, recv],
            device_id=where, device_id_type=MESH,
        )

    def local_copy(c):
        return pltpu.make_async_copy(
            jac.at[:, pl.ds(pl.multiple_of(c * wide, wide), wide)], cols.at[c], sem_local.at[c]
        )

    def far_copy(c):
        return remote(cols.at[c], far.at[c], sem_far, back_two, c, c)

    def near_copy(c, src):
        return remote(src.at[c], near.at[c], sem_near, partner, c, c)

    def core_copy(u):
        return remote(csend.at[u], crecv.at[u], sem_core, other_core, u, u)

    def side_copy(u):
        return remote(xsend.at[u], xrecv.at[u], sem_x, other_side, u, u)

    def each(count, body):
        def step(i, carry):
            body(i)
            return carry

        lax.fori_loop(0, count, step, 0)

    each(chunks, lambda c: local_copy(c).start())
    std_row[...] = rows_in[1:2, :]
    barrier = pltpu.get_barrier_semaphore()

    def greet_state(d):
        to = lax.rem(block + 1 + d, n_state)
        pl.semaphore_signal(barrier, inc=1, device_id={"state": to}, device_id_type=MESH)

    def greet_obs(d):
        to = lax.rem(group + 1 + d, n_obs)
        pl.semaphore_signal(barrier, inc=1, device_id={"obs": to}, device_id_type=MESH)

    each(n_state - 1, greet_state)
    each(n_obs - 1, greet_obs)
    pl.semaphore_wait(barrier, n_state - 1 + n_obs - 1)

    def launch(c):
        far_copy(c).start()

        @pl.when(odd == 1)
        def _():
            near_copy(c, cols).start()

    local_copy(0).wait()
    launch(0)
    local_copy(1).wait()
    launch(1)
    each(chunks - 2, lambda c: local_copy(c + 2).wait())
    std_near = remote(std_row, std_in.at[0], sem_std, back_one, 0, 0)
    std_far = remote(std_row, std_in.at[1], sem_std, back_two, 1, 1)
    std_near.start()
    std_far.start()

    parts = rows // wide

    def turn(i):
        c = i // parts
        r = pl.multiple_of(lax.rem(i, parts) * wide, wide)
        across = pl.ds(r, wide)
        down = pl.ds(pl.multiple_of(c * wide, wide), wide)
        tile = cols[c, across, :].astype(F32).T
        turned[down, across] = (tile * weight[:, across]).astype(BF16)
        lead = jnp.broadcast_to(rows_in[0:1, down], (16, wide)).astype(BF16)
        piece = nn(lead, tile.astype(BF16))[:1]

        @pl.when(c == 0)
        def _():
            model[:, across] = piece

        @pl.when(c > 0)
        def _():
            model[:, across] += piece

    each(chunks * parts, turn)

    def upright(c):
        at = pl.ds(pl.multiple_of(c * wide, wide), wide)
        std_col[at, :] = jnp.broadcast_to(std_row[:, at], (std_col.shape[1], wide)).T

    each(chunks, upright)

    def model_copy(d):
        to = lax.rem(block + 1 + d, n_state)
        return remote(model, model_in.at[block], sem_model, {"state": to}, d, block)

    def model_landed(d):
        of = lax.rem(block + 1 + d, n_state)
        return remote(model, model_in.at[of], sem_model, {"state": of}, d, of)

    each(n_state - 1, lambda d: model_copy(d).start())

    def multiply(src, u):
        def given(h):
            q = 2 * h + 1 - core
            left = turned[pl.ds(pl.multiple_of(q * quarter, quarter), quarter), :]
            csend[u, h] = nn(left, src[...]).astype(BF16)

        def kept(h):
            q = 2 * h + core
            left = turned[pl.ds(pl.multiple_of(q * quarter, quarter), quarter), :]
            keep[u, h] = nn(left, src[...])

        each(2, given)
        core_copy(u).start()
        each(2, kept)

    def pass_on(u):
        core_copy(u).wait_recv()
        xsend[u] = (keep[u, 1 - side] + crecv[u, 1 - side].astype(F32)).astype(BF16)
        side_copy(u).start()
        keep[u, side] += crecv[u, side].astype(F32)

    my_rows = std_col[pl.ds(pl.multiple_of(group * quarter, quarter), quarter), 0:1]

    def finish(u, k, c):
        side_copy(u).wait_recv()
        at = pl.ds(pl.multiple_of(c * wide, wide), wide)
        if k == 0:
            scale = std_row[:, at]
        else:
            scale = std_in[k - 1, :, at]
        band[k, :, at] = (keep[u, side] + xrecv[u].astype(F32)) * my_rows * scale

    def descent_copy(d):
        to = lax.rem(group + 1 + d, n_obs)
        return remote(descent, descent_in.at[group], sem_descent, {"obs": to}, d, group)

    def descent_landed(d):
        of = lax.rem(group + 1 + d, n_obs)
        return remote(descent, descent_in.at[of], sem_descent, {"obs": of}, d, of)

    def dense_copy(d):
        to = lax.rem(block + 1 + d, n_state)
        return remote(dense.at[to], dense_in.at[block], sem_dense, {"state": to}, d, block)

    def dense_landed(d):
        of = lax.rem(block + 1 + d, n_state)
        return remote(dense.at[of], dense_in.at[of], sem_dense, {"state": of}, d, of)

    def do_misfit():
        each(n_state - 1, lambda d: model_landed(d).wait_recv())
        model_in[block] = model[...]
        total = jnp.sum(model_in[...], axis=0)
        misfit = (weight[...] * (observed[...] - total)).astype(BF16)
        lead = jnp.broadcast_to(misfit, (16, rows))

        def part(c):
            at = pl.ds(pl.multiple_of(c * wide, wide), wide)
            descent[:, at] = nn(lead, cols[c])[:1]

        each(chunks, part)
        each(n_obs - 1, lambda d: descent_copy(d).start())

    def do_owners():
        each(n_obs - 1, lambda d: descent_landed(d).wait_recv())
        descent_in[group] = descent[...]
        scaled = std_row[...] * jnp.sum(descent_in[...], axis=0)
        high = scaled.astype(BF16).astype(F32)
        rest = scaled - high
        middle = rest.astype(BF16).astype(F32)
        low = rest - middle
        index = lax.broadcasted_iota(jnp.int32, (16, width), 0)
        three = jnp.where(
            index == 0, high, jnp.where(index == 1, middle, jnp.where(index == 2, low, 0.0))
        ).astype(BF16)
        place = lax.broadcasted_iota(jnp.int32, (wide, width), 0)

        def spread(i):
            t = i // chunks
            c = lax.rem(i, chunks)
            hot = jnp.where(rows_in[2:3, :] == (place + i * wide).astype(F32), 1.0, 0.0).astype(BF16)
            at = pl.ds(pl.multiple_of(c * wide, wide), wide)
            dense[t, :, at] = jnp.sum(nt(three, hot), axis=0, keepdims=True)

        each(n_state * chunks, spread)
        each(n_state - 1, lambda d: dense_copy(d).start())

    def of_far(c):
        return 3 * c

    def of_own(c):
        return 3 * c + 1

    def of_near(c):
        return 3 * c + 2

    def arrivals(j):
        @pl.when(jnp.logical_and(j >= 2, j + 2 < chunks))
        def _():
            far_copy(j).wait_send()
            launch(j + 2)

        far_copy(j).wait_recv()

        @pl.when(odd == 0)
        def _():
            near_copy(j, far).start()


        multiply(far.at[j], of_far(j))

        @pl.when(j == 0)
        def _():
            std_near.wait_recv()
            std_far.wait_recv()

        @pl.when(j == 1)
        def _():
            pass_on(of_own(0))

        @pl.when(j >= 2)
        def _():
            pass_on(of_near(j - 2))

        @pl.when(j >= 1)
        def _():
            finish(of_far(j - 1), 2, j - 1)

        multiply(cols.at[j], of_own(j))
        pass_on(of_far(j))

        @pl.when(j >= 1)
        def _():
            finish(of_own(j - 1), 0, j - 1)
            near_copy(j - 1, cols).wait_recv()
            multiply(near.at[j - 1], of_near(j - 1))
            pass_on(of_own(j))

        @pl.when(j >= 2)
        def _():
            finish(of_near(j - 2), 1, j - 2)

        @pl.when(j == 0)
        def _():
            do_owners()

    def follow(c):
        far_copy(c).wait_send()
        launch(c + 2)

    do_misfit()
    each(2, follow)
    each(chunks, arrivals)
    last = chunks - 1
    pass_on(of_near(last - 1))
    finish(of_far(last), 2, last)
    finish(of_own(last), 0, last)
    each(n_state - 1, lambda d: dense_landed(d).wait_recv())
    dense_in[block] = dense[block]
    gradient[...] = jnp.sum(dense_in[...], axis=0)
    near_copy(last, cols).wait_recv()
    multiply(near.at[last], of_near(last))
    finish(of_near(last - 1), 1, last - 1)
    pass_on(of_near(last))
    finish(of_near(last), 1, last)

    def sent(c):
        near_copy(c, cols).wait_send()

    each(chunks, sent)
    far_copy(chunks - 2).wait_send()
    far_copy(chunks - 1).wait_send()
    each(units, lambda u: core_copy(u).wait_send())
    each(units, lambda u: side_copy(u).wait_send())
    each(n_state - 1, lambda d: model_copy(d).wait_send())
    each(n_state - 1, lambda d: dense_copy(d).wait_send())
    each(n_obs - 1, lambda d: descent_copy(d).wait_send())
    std_near.wait_send()
    std_far.wait_send()


def on_device(n_obs, n_state, jacobian, obs_weight, observed, prior_state, prior_std, owner_slot):
    rows, width = jacobian.shape
    quarter = width // n_obs
    chunks = width // CHUNK
    units = 3 * chunks
    vmem = pl.BlockSpec(memory_space=pltpu.VMEM)
    dma = pltpu.SemaphoreType.DMA
    band, gradient = pl.pallas_call(
        functools.partial(kernel, n_obs, n_state),
        out_shape=(
            jax.ShapeDtypeStruct((3, quarter, width), F32),
            jax.ShapeDtypeStruct((1, width), F32),
        ),
        in_specs=[pl.BlockSpec(memory_space=pl.ANY)] + [vmem] * 3,
        out_specs=(vmem, vmem),
        scratch_shapes=[
            pltpu.VMEM((chunks, rows, CHUNK), BF16),
            pltpu.VMEM((width, rows), BF16),
            pltpu.VMEM((chunks, rows, CHUNK), BF16),
            pltpu.VMEM((chunks, rows, CHUNK), BF16),
            pltpu.VMEM((units, 2, quarter, CHUNK), BF16),
            pltpu.VMEM((units, 2, quarter, CHUNK), BF16),
            pltpu.VMEM((units, 2, quarter, CHUNK), F32),
            pltpu.VMEM((units, quarter, CHUNK), BF16),
            pltpu.VMEM((units, quarter, CHUNK), BF16),
            pltpu.VMEM((1, rows), F32),
            pltpu.VMEM((n_state, 1, rows), F32),
            pltpu.VMEM((1, width), F32),
            pltpu.VMEM((n_obs, 1, width), F32),
            pltpu.VMEM((n_state, 1, width), F32),
            pltpu.VMEM((n_state, 1, width), F32),
            pltpu.VMEM((2, 1, width), F32),
            pltpu.VMEM((1, width), F32),
            pltpu.VMEM((width, 128), F32),
            dma((chunks,)),
            dma((2, chunks)),
            dma((2, chunks)),
            dma((2, units)),
            dma((2, units)),
            dma((2, n_state)),
            dma((2, n_obs)),
            dma((2, n_state)),
            dma((2, 2)),
        ],
        compiler_params=pltpu.CompilerParams(
            collective_id=0, has_side_effects=True, vmem_limit_bytes=60 * 1024 * 1024
        ),
        cost_estimate=pl.CostEstimate(
            flops=6 * rows * width * width, bytes_accessed=10 * rows * width, transcendentals=0
        ),
        name="band_and_gradient",
    )(
        jacobian, obs_weight[None, :], observed[None, :],
        jnp.stack([prior_state.astype(F32), prior_std.astype(F32), owner_slot.astype(F32)]),
    )
    return jnp.transpose(band, (1, 0, 2))[None], gradient[0]


def solution(mesh):
    n_obs, n_state = mesh.shape["obs"], mesh.shape["state"]
    assert n_obs == 4 and n_state % 2 == 0
    placed = (P("obs", "state"), P("obs"), P("obs"), P("state"), P("state"), P("state"))
    return jax.shard_map(
        functools.partial(on_device, n_obs, n_state),
        mesh=mesh,
        in_specs=placed,
        out_specs=(P("state", "obs", None, None), P("state")),
        check_vma=False,
    )
```
